32 devices in a mesh: expert: 16 (over z, y, x), half: 2 (over core).
Axes of the slice: x: 2, y: 2, z: 4, core: 2. Of those that a mesh axis runs over, the one named last changes fastest.
Arguments:
- hidden_in: bfloat16 [2048, 2048], P('expert'), may hold values from -6 to 6
- modality: int32 [2048], replicated, may hold values from 0 to 1, as said below
- expert_ids: int32 [2048, 8], P('expert'), may hold values from 0 to 15, all different within a row; in each aligned block of 128 rows (0 to 127, 128 to 255, ...) at most 96 rows name the same one
- route_weights: float32 [2048, 8], P('expert'), may hold values from 0.03 to 0.3
- w_gate_up: bfloat16 [32, 2048, 2, 768], P('expert', None, None, 'half'), may hold values from -0.125 to 0.125
- w_down: bfloat16 [32, 768, 2048], P('expert', 'half'), may hold values from -0.21875 to 0.21875
- norm_gain: float32 [2048], replicated, may hold values from 0.1 to 1.9
- w_query: bfloat16 [2048, 4096], P(None, 'half'), may hold values from -1 to 1
- key_value_weight: bfloat16 [2048, 2, 512], P(None, None, 'half'), may hold values from -1 to 1
- q_gain: float32 [128], replicated, may hold values from 1 to 8
- k_gain: float32 [128], replicated, may hold values from 1 to 8
Outputs:
- hidden_out: float32 [2048, 2048], P('expert')
- attended: bfloat16 [2048, 4096], P('expert', 'half')
The draws below stay inside these ranges and needn't reach their ends.
Inputs may be any that keep to these rules, and one draw needn't show every extreme that they name: `modality`: constant over each aligned block of 128 tokens; both values occur. `expert_ids`: the 8 ids of a token differ; among the tokens of one aligned block of 128 no id is named more than 96 times, a bound that some block reaches.
All inputs are finite; a program needn't handle non-finite values.
Results may differ from the reference program's by a relative error of at most 0.03.
The reference program's roundings to bfloat16 on the way count: a program that leaves them out, or rounds other values in their place, can miss the bound.
Values may be sent and summed in bfloat16 or wider, within the bound.
No kernel may reach another device: no remote copies, remote signals or barrier semaphores. Data moves between devices by JAX's collectives and lax.ppermute only.
A program may use at most 128 MiB of HBM per device.

```python
import math
import jax
import jax.numpy as jnp
import numpy as np
from jax import lax

MODEL_DIMENSION = 2048
FF = 768
QUERY_HEADS = 32
KEY_VALUE_HEADS = 4
HEAD_SIZE = 128
TOPK = 8
EXP_DEV = 2
TOK_DEV = 128
EXPERTS = 32
SEQUENCE_TOKENS = 2048
CAP = 96
N_EXPERT = 16
N_HALF = 2


def query_start(key):
    return jax.random.normal(jax.random.fold_in(key, 11), (MODEL_DIMENSION, QUERY_HEADS * HEAD_SIZE), jnp.float32) * MODEL_DIMENSION ** (-0.5)


def draw_w_query(key, part):
    return query_start(key).astype(jnp.bfloat16)


def draw_key_value_weight(key, part):
    key_portion = jax.random.normal(jax.random.fold_in(key, 12), (MODEL_DIMENSION, KEY_VALUE_HEADS * HEAD_SIZE), jnp.float32) * MODEL_DIMENSION ** (-0.5)
    value_portion = jax.random.normal(jax.random.fold_in(key, 13), (MODEL_DIMENSION, KEY_VALUE_HEADS * HEAD_SIZE), jnp.float32) * MODEL_DIMENSION ** (-0.5)
    return jnp.stack([key_portion, value_portion], axis=1).astype(jnp.bfloat16)


def gain_draw(key, salt):
    return jnp.exp(jax.random.uniform(jax.random.fold_in(key, salt), (HEAD_SIZE,), jnp.float32, 0.0, math.log(4.0)))


def draw_q_gain(key, part):
    return gain_draw(key, 21)


def draw_k_gain(key, part):
    return gain_draw(key, 22)


def draw_modality(key, part):
    block_count = SEQUENCE_TOKENS // TOK_DEV
    picks = jax.random.randint(jax.random.fold_in(key, 31), (block_count,), 0, 10)
    kinds = (picks < 7).astype(jnp.int32)
    kinds = kinds.at[0].set(0).at[1].set(1)
    return jnp.repeat(kinds, TOK_DEV, total_repeat_length=SEQUENCE_TOKENS)


def steps_of(own_key, dims, split, least, largest):
    def one(position, shards_of):
        steps = jax.random.uniform(jax.random.fold_in(jax.random.fold_in(own_key, 6), position), (shards_of,), jnp.float32, least / len(split), largest / len(split))
        return jnp.repeat(jnp.exp(steps), dims[position] // shards_of).reshape((-1,) + (1,) * (len(dims) - position - 1))

    level = one(*split[0])
    for cut in split[1:]:
        level = level * one(*cut)
    return level


def deal_out(own_key, own, number, rows, count, top, most, lean):
    order = jax.random.permutation(own_key, count)
    packed, common = portions_of(count, rows * top, most, lean, True), portions_of(count, rows * top, most, lean, False)
    places = jnp.arange(count)

    def named(sizes, rotation):
        used = int((sizes > 0).sum())
        fixed = max(1, used // 4)
        passed = fixed + (places - fixed + rotation * (used - fixed)) % max(1, count - fixed)
        return jnp.zeros((count,), jnp.int32).at[order[jnp.where(places < fixed, places, passed)]].set(jnp.asarray(sizes, jnp.int32))

    sizes = jnp.where(number % 4 == 0, named(packed, number // 4), named(common, number - number // 4 - 1))
    mixed = jax.random.permutation(jax.random.fold_in(own, 3), count)
    giver, taker = mixed[0:count // 2 * 2:2], mixed[1:count // 2 * 2:2]
    room = jnp.minimum(sizes[giver] - 1, most - sizes[taker]) // 2
    room = jnp.where((giver == order[0]) | (taker == order[0]) | (sizes[taker] == 0), 0, jnp.maximum(room, 0))
    passed = jax.random.randint(jax.random.fold_in(own, 4), (count // 2,), 0, 1 << 20) % (room + 1)
    sizes = sizes.at[giver].add(-passed).at[taker].add(passed)
    items = jnp.searchsorted(jnp.cumsum(sizes), jnp.arange(rows * top), side="right").astype(jnp.int32)
    grid = items.reshape(top, rows).T
    grid = grid[jax.random.permutation(jax.random.fold_in(own, 1), rows)]
    rotation = jax.random.randint(jax.random.fold_in(own, 2), (rows, 1), 0, top)
    return jnp.take_along_axis(grid, (jnp.arange(top)[None, :] + rotation) % top, axis=1)


def portions_of(count, total, reach, slope, full):
    weights = [(1 << 20) // math.isqrt(standing ** slope) + 1 for standing in range(1, count + 1)]
    largest = reach if full else min(reach, max(-(-total // count), total * weights[0] // sum(weights)))
    least = 1 if total - largest >= count - 1 else 0
    holding, surplus = [largest] + [least] * (count - 1), total - largest - least * (count - 1)
    while surplus > 0:
        free = [i for i in range(1, count) if holding[i] < largest] or [i for i in range(1, count) if holding[i] < reach]
        mass, remaining = sum([weights[i] for i in free]), surplus
        for i in free:
            more = min(reach - holding[i], max(1, remaining * weights[i] // mass), surplus)
            holding[i] = holding[i] + more
            surplus = surplus - more
    return np.array(holding)


def scatter_about(stream_key, shape, deviation, limit, split=(), kind=jnp.bfloat16):
    loudness = steps_of(stream_key, shape, split, -0.22, 0.18) if split else 1.0
    values = jax.random.normal(stream_key, shape, jnp.float32) * deviation * loudness
    return jnp.minimum(jnp.maximum(values, -limit), limit).astype(kind)


def setup_inputs(seed: int = 0) -> dict:
    splits = jax.random.split(jax.random.key(seed), 12)
    hidden_in = scatter_about(splits[0], (SEQUENCE_TOKENS, MODEL_DIMENSION), 1.0, 6.0, ((0, 16),))
    modality = draw_modality(jax.random.fold_in(splits[11], 71), 0)
    expert_ids_keys = jax.random.split(jax.random.fold_in(splits[2], 1), SEQUENCE_TOKENS // TOK_DEV)
    expert_ids_turns = jax.random.permutation(jax.random.fold_in(splits[2], 3), SEQUENCE_TOKENS // TOK_DEV)
    expert_ids = jax.vmap(lambda own, number: deal_out(jax.random.fold_in(splits[2], 2), own, number, TOK_DEV, N_EXPERT, TOPK, CAP, 2))(expert_ids_keys, expert_ids_turns).reshape((SEQUENCE_TOKENS, TOPK))
    route_weights = jnp.clip(jnp.exp(math.log(0.3) - 2.3025852 * jax.random.uniform(splits[3], (SEQUENCE_TOKENS, TOPK), jnp.float32) ** steps_of(splits[3], (SEQUENCE_TOKENS, TOPK), ((0, 16),), -0.2, 0.2)), 0.03, 0.3)
    w_gate_up = scatter_about(splits[4], (EXPERTS, MODEL_DIMENSION, 2, FF), MODEL_DIMENSION ** -0.5, 0.125, ((0, 16), (3, 2)))
    w_down = scatter_about(splits[5], (EXPERTS, FF, MODEL_DIMENSION), FF ** -0.5, 0.21875, ((0, 16), (1, 2)))
    norm_gain = jnp.clip(1.0 + 0.18 * jax.random.normal(splits[6], (MODEL_DIMENSION,), jnp.float32), 0.1, 1.9)
    w_query = draw_w_query(jax.random.fold_in(splits[11], 71), 0)
    key_value_weight = draw_key_value_weight(jax.random.fold_in(splits[11], 71), 0)
    q_gain = draw_q_gain(jax.random.fold_in(splits[11], 71), 0)
    k_gain = draw_k_gain(jax.random.fold_in(splits[11], 71), 0)
    return dict(hidden_in=hidden_in, modality=modality, expert_ids=expert_ids, route_weights=route_weights, w_gate_up=w_gate_up, w_down=w_down, norm_gain=norm_gain, w_query=w_query, key_value_weight=key_value_weight, q_gain=q_gain, k_gain=k_gain)


EPSILON = 1e-06
tile_rows = 128

def rms_scale(values, gain_row):
    mean_sq = lax.optimization_barrier(jnp.mean(values * values, axis=-1, keepdims=True))
    return values * lax.rsqrt(mean_sq + EPSILON) * gain_row

def moe_block(hidden_in, modality, expert_ids, route_weights, w_gate_up, w_down):
    row_count = SEQUENCE_TOKENS * TOPK
    flat_expert = (EXP_DEV * expert_ids + modality[:, None]).reshape(-1).astype(jnp.int32)
    ordering = jnp.argsort(flat_expert, stable=True).astype(jnp.int32)
    sorted_expert = flat_expert[ordering]
    counts = jnp.zeros((EXPERTS,), jnp.int32).at[flat_expert].add(1)
    starts = (jnp.cumsum(counts) - counts).astype(jnp.int32)
    padded = ((counts + tile_rows - 1) // tile_rows * tile_rows).astype(jnp.int32)
    padded_end = jnp.cumsum(padded).astype(jnp.int32)
    padded_start = (padded_end - padded).astype(jnp.int32)
    positions = (padded_start[sorted_expert] + jnp.arange(row_count, dtype=jnp.int32) - starts[sorted_expert]).astype(jnp.int32)
    tile_count = row_count // tile_rows + 1 + EXPERTS
    source_token = jnp.full((tile_count * tile_rows,), SEQUENCE_TOKENS, jnp.int32).at[positions].set((ordering // TOPK).astype(jnp.int32))
    tile_first = (jnp.arange(tile_count, dtype=jnp.int32) * tile_rows)[:, None]
    tile_expert = jnp.minimum(lax.optimization_barrier(jnp.sum((padded_end[None, :] <= tile_first).astype(jnp.int32), axis=1)), EXPERTS - 1).astype(jnp.int32)
    padded_in = jnp.concatenate([hidden_in, jnp.zeros((1, MODEL_DIMENSION), hidden_in.dtype)], axis=0)
    half_units = FF // N_HALF

    def one_tile(tile_args):
        tile_tokens, expert = tile_args
        rows_in = padded_in[tile_tokens]
        weights_gu = w_gate_up[expert]
        gate_part = jnp.dot(rows_in, weights_gu[:, 0, :], preferred_element_type=jnp.float32)
        upward = jnp.dot(rows_in, weights_gu[:, 1, :], preferred_element_type=jnp.float32)
        activated = (jax.nn.silu(gate_part) * upward).astype(jnp.bfloat16)
        down_rows = w_down[expert]
        summed = jnp.zeros((tile_rows, MODEL_DIMENSION), jnp.float32)
        for half_index in range(N_HALF):
            lower = half_index * half_units
            summed = summed + jnp.dot(activated[:, lower:lower + half_units], down_rows[lower:lower + half_units], preferred_element_type=jnp.float32)
        return summed.astype(jnp.bfloat16)
    tile_out = lax.map(one_tile, (source_token.reshape(tile_count, tile_rows), tile_expert)).reshape(tile_count * tile_rows, MODEL_DIMENSION)
    row_position = jnp.zeros((row_count,), jnp.int32).at[ordering].set(positions)
    routed = tile_out[row_position].astype(jnp.float32).reshape(SEQUENCE_TOKENS, TOPK, MODEL_DIMENSION)
    mixture = lax.optimization_barrier(jnp.sum(routed * route_weights[:, :, None], axis=1))
    return hidden_in.astype(jnp.float32) + mixture

def attention(hidden_out, norm_gain, w_query, key_value_weight, q_gain, k_gain):
    normalized_input = rms_scale(hidden_out, norm_gain).astype(jnp.bfloat16)
    queries = jnp.dot(normalized_input, w_query, preferred_element_type=jnp.float32).reshape(SEQUENCE_TOKENS, QUERY_HEADS, HEAD_SIZE)
    queries = rms_scale(queries, q_gain).astype(jnp.bfloat16)
    key_value_rows = jnp.dot(normalized_input, key_value_weight.reshape(MODEL_DIMENSION, 2 * KEY_VALUE_HEADS * HEAD_SIZE), preferred_element_type=jnp.float32).reshape(SEQUENCE_TOKENS, 2, KEY_VALUE_HEADS, HEAD_SIZE)
    keys_wide = rms_scale(key_value_rows[:, 0], k_gain).astype(jnp.bfloat16).astype(jnp.float32)
    values_wide = key_value_rows[:, 1].astype(jnp.bfloat16).astype(jnp.float32)
    queries_per_group = QUERY_HEADS // KEY_VALUE_HEADS
    rows_per_block = math.gcd(SEQUENCE_TOKENS, 256)
    score_scale = HEAD_SIZE ** (-0.5)

    def one_block(query_tile_rows):
        grouped_queries = query_tile_rows.astype(jnp.float32).reshape(rows_per_block, KEY_VALUE_HEADS, queries_per_group, HEAD_SIZE)
        scores = jnp.einsum('qhgd,khd->hgqk', grouped_queries, keys_wide) * score_scale
        row_peak = lax.optimization_barrier(jnp.max(scores, axis=-1, keepdims=True))
        weights = jnp.exp(scores - row_peak)
        totals = lax.optimization_barrier(jnp.sum(weights, axis=-1, keepdims=True))
        rounded_probs = lax.optimization_barrier(weights.astype(jnp.bfloat16)).astype(jnp.float32)
        mixed_rows = jnp.einsum('hgqk,khd->hgqd', rounded_probs, values_wide) / totals
        return mixed_rows.transpose(2, 0, 1, 3).reshape(rows_per_block, QUERY_HEADS * HEAD_SIZE).astype(jnp.bfloat16)
    attended = lax.map(one_block, queries.reshape(SEQUENCE_TOKENS // rows_per_block, rows_per_block, QUERY_HEADS, HEAD_SIZE))
    return attended.reshape(SEQUENCE_TOKENS, QUERY_HEADS * HEAD_SIZE)

def reference(hidden_in, modality, expert_ids, route_weights, w_gate_up, w_down, norm_gain, w_query, key_value_weight, q_gain, k_gain):
    hidden_out = moe_block(hidden_in, modality, expert_ids, route_weights, w_gate_up, w_down)
    attended = attention(hidden_out, norm_gain, w_query, key_value_weight, q_gain, k_gain)
    return (hidden_out, attended)
```

```python
import functools

import jax
import jax.numpy as jnp
from jax import lax
from jax.experimental import pallas as pl
from jax.experimental.pallas import tpu as pltpu
from jax.sharding import PartitionSpec as P

EPSILON = 1e-06
LANES = 128
KEYS_AT_ONCE = 2048
MIB = 1024 * 1024


def rms_scale(values, gain_row):
    mean_sq = jnp.mean(values * values, axis=-1, keepdims=True)
    return values * lax.rsqrt(mean_sq + EPSILON) * gain_row


def swap(value, mask_first, mask_second):
    pairs = []
    for expert in range(lax.axis_size("expert")):
        for half, mask in enumerate((mask_first, mask_second)):
            pairs.append((2 * expert + half, 2 * (expert ^ mask) + half))
    return lax.ppermute(value, ("expert", "half"), pairs)


def swap_half(value):
    return lax.ppermute(value, "half", [(0, 1), (1, 0)])


def expert_kernel(
    block_rows,
    kinds_ref,
    x_ref,
    pick_ref,
    own_gu,
    other_gu,
    own_down,
    other_down,
    keep_ref,
    send_ref,
    gu_ref,
    down_ref,
    act_ref,
    sems,
):
    width = own_down.shape[2]
    units = own_down.shape[1]
    tiles = x_ref.shape[0] // (4 * block_rows)
    copies = []
    for m in range(2):
        for k, (gu, down) in enumerate(((own_gu, own_down), (other_gu, other_down))):
            group = [
                pltpu.make_async_copy(
                    gu.at[m, c], gu_ref.at[m, k, :, pl.ds(c * units, units)], sems.at[m, k, c]
                )
                for c in range(2)
            ]
            group.append(
                pltpu.make_async_copy(
                    down.at[m], down_ref.at[m, pl.ds(k * units, units)], sems.at[m, k, 2]
                )
            )
            copies.append(group)
            for copy in group:
                copy.start()
    tile_rows = 4 * block_rows
    for m in range(2):
        for k in range(2):
            for copy in copies[2 * m + k]:
                copy.wait()
        for tile in range(tiles):
            rows = pl.ds(tile * tile_rows, tile_rows)
            kinds = [kinds_ref[4 * tile + p] for p in range(4)]
            row_block = lax.broadcasted_iota(jnp.int32, (tile_rows, 1), 0) // block_rows
            row_kind = jnp.where(
                row_block == 0,
                kinds[0],
                jnp.where(row_block == 1, kinds[1], jnp.where(row_block == 2, kinds[2], kinds[3])),
            )
            used = sum((kind == m).astype(jnp.int32) for kind in kinds) > 0
            half_tiles = tiles // 2 if tiles > 1 else 0

            def store(value, ref, at, count, row_at):
                mine = row_kind[row_at : row_at + count] == m
                if m == 0:
                    ref[at : at + count] = jnp.where(mine, value, 0.0).astype(ref.dtype)
                else:
                    before = ref[at : at + count].astype(jnp.float32)
                    ref[at : at + count] = jnp.where(mine, value, before).astype(ref.dtype)

            def place(value):
                if tiles == 1:
                    cut = tile_rows // 2
                    store(value[:cut], keep_ref, 0, cut, 0)
                    store(value[cut:], send_ref, 0, cut, cut)
                elif tile < half_tiles:
                    store(value, keep_ref, tile * tile_rows, tile_rows, 0)
                else:
                    store(value, send_ref, (tile - half_tiles) * tile_rows, tile_rows, 0)

            @pl.when(used)
            def _():
                x = x_ref[rows, :width]
                extra = x_ref[rows, width:].astype(jnp.float32)
                weight = jnp.sum(extra * pick_ref[...], axis=-1, keepdims=True)
                for k in range(2):
                    pre = jnp.dot(x, gu_ref[m, k], preferred_element_type=jnp.float32)
                    gate, up = pre[:, :units], pre[:, units:]
                    act = gate / (1.0 + jnp.exp(-gate)) * up
                    act_ref[:, k * units : (k + 1) * units] = act.astype(jnp.bfloat16)
                out = jnp.dot(act_ref[...], down_ref[m], preferred_element_type=jnp.float32)
                place(out.astype(jnp.bfloat16).astype(jnp.float32) * weight)

            if m == 0:

                @pl.when(jnp.logical_not(used))
                def _():
                    place(jnp.zeros((tile_rows, width), jnp.float32))


def expert_call(kinds, rows, pick, own_gu, other_gu, own_down, other_down, block_rows):
    total = rows.shape[0]
    _, units, width = own_down.shape
    half = total // 2
    vmem, anywhere = pl.BlockSpec(memory_space=pltpu.VMEM), pl.BlockSpec(memory_space=pl.ANY)
    return pl.pallas_call(
        functools.partial(expert_kernel, block_rows),
        out_shape=(
            jax.ShapeDtypeStruct((half, width), jnp.float32),
            jax.ShapeDtypeStruct((half, width), jnp.bfloat16),
        ),
        in_specs=[pl.BlockSpec(memory_space=pltpu.SMEM), vmem, vmem] + [anywhere] * 4,
        out_specs=(vmem, vmem),
        scratch_shapes=[
            pltpu.VMEM((2, 2, width, 2 * units), jnp.bfloat16),
            pltpu.VMEM((2, 2 * units, width), jnp.bfloat16),
            pltpu.VMEM((4 * block_rows, 2 * units), jnp.bfloat16),
            pltpu.SemaphoreType.DMA((2, 2, 3)),
        ],
        compiler_params=pltpu.CompilerParams(vmem_limit_bytes=48 * MIB),
        cost_estimate=pl.CostEstimate(
            flops=2 * total * width * 6 * units * 2,
            bytes_accessed=2 * 2 * 6 * units * width,
            transcendentals=total * units * 4,
        ),
        name="experts",
    )(kinds, rows, pick, own_gu, other_gu, own_down, other_down)


def attention_kernel(head_dim, group, q_ref, *refs):
    kv_refs, out_ref = refs[:-1], refs[-1]
    kv_heads = kv_refs[0].shape[1] // (2 * head_dim)
    scale = head_dim**-0.5
    rows = q_ref.shape[0]
    step = max(1, KEYS_AT_ONCE // kv_refs[0].shape[0])
    def columns(ref, head, count=1):
        return ref[:, pl.ds(pl.multiple_of(head * head_dim, head_dim), count * head_dim)]

    def two_heads(pair, carry):
        g = pair // (group // 2)
        both = columns(q_ref, 2 * pair, 2)
        q = jnp.concatenate([both[:, :head_dim], both[:, head_dim:]], axis=0)
        keys = [columns(ref, g) for ref in kv_refs]
        vals = [columns(ref, kv_heads + g) for ref in kv_refs]
        peak, total, mixed = None, 0.0, 0.0
        for at in range(0, len(keys), step):
            scores = [
                lax.dot_general(q, k, (((1,), (1,)), ((), ())), preferred_element_type=jnp.float32)
                for k in keys[at : at + step]
            ]
            peaks = [jnp.max(s, axis=-1, keepdims=True) for s in scores]
            if peak is not None:
                before = peak
                peak = functools.reduce(jnp.maximum, peaks + [before])
                shrink = jnp.exp((before - peak) * scale)
                total, mixed = total * shrink, mixed * shrink
            else:
                peak = functools.reduce(jnp.maximum, peaks)
            for s, v in zip(scores, vals[at : at + step]):
                p = jnp.exp((s - peak) * scale)
                total = total + jnp.sum(p, axis=-1, keepdims=True)
                mixed = mixed + jnp.dot(
                    p.astype(jnp.bfloat16), v, preferred_element_type=jnp.float32
                )
        mixed = (mixed / total).astype(jnp.bfloat16)
        at = pl.multiple_of(2 * pair * head_dim, 2 * head_dim)
        out_ref[:, pl.ds(at, 2 * head_dim)] = jnp.concatenate([mixed[:rows], mixed[rows:]], axis=1)
        return carry

    lax.fori_loop(0, kv_heads * group // 2, two_heads, 0)


def attention_call(queries, kv_parts, head_dim, group):
    vmem = pl.BlockSpec(memory_space=pltpu.VMEM)
    rows, width = queries.shape
    keys = sum(part.shape[0] for part in kv_parts)
    return pl.pallas_call(
        functools.partial(attention_kernel, head_dim, group),
        out_shape=jax.ShapeDtypeStruct((rows, width), jnp.bfloat16),
        in_specs=[vmem] * (1 + len(kv_parts)),
        out_specs=vmem,
        compiler_params=pltpu.CompilerParams(vmem_limit_bytes=48 * MIB),
        cost_estimate=pl.CostEstimate(
            flops=4 * rows * keys * width,
            bytes_accessed=4 * rows * width,
            transcendentals=rows * keys * width // head_dim,
        ),
        name="attention",
    )(queries, *kv_parts)


def body(
    hidden_in,
    modality,
    expert_ids,
    route_weights,
    w_gate_up,
    w_down,
    norm_gain,
    w_query,
    key_value_weight,
    q_gain,
    k_gain,
):
    tok_rows, model_width = hidden_in.shape
    groups = lax.axis_size("expert")
    me, core = lax.axis_index("expert"), lax.axis_index("half")
    block_rows = tok_rows // 2
    slots = groups // 4
    per_group = max(1, slots // 4)
    slot_groups = [list(range(s, s + per_group)) for s in range(0, slots, per_group)]

    own_gu = w_gate_up.transpose(0, 2, 1, 3)
    other_down = swap_half(w_down)
    other_gu = swap_half(own_gu)

    chosen = expert_ids[:, :, None] == jnp.arange(groups, dtype=jnp.int32)
    table = jnp.sum(jnp.where(chosen, route_weights[:, :, None], 0.0), axis=1)
    table_high = table.astype(jnp.bfloat16)
    table_low = (table - table_high.astype(jnp.float32)).astype(jnp.bfloat16)
    extra = [table_high, table_low]
    if 2 * groups < LANES:
        extra.append(jnp.zeros((tok_rows, LANES - 2 * groups), jnp.bfloat16))
    payload = jnp.concatenate([hidden_in] + extra, axis=1)
    payload = lax.dynamic_slice_in_dim(payload, core * block_rows, block_rows, 0)
    lane = jnp.arange(LANES, dtype=jnp.int32)
    pick = ((lane == me) | (lane == me + groups)).astype(jnp.float32)[None, :]

    kind_of = modality.reshape(groups, tok_rows)[:, 0]
    near = jnp.where(core == 0, jnp.array([0, 1, 2, 3], jnp.int32), jnp.array([0, 2, 1, 3], jnp.int32))

    arrived = {0: payload}
    for s in range(1, slots):
        arrived[s] = swap(payload, 4 * s, 4 * s)
    returned = {}
    for members in slot_groups:
        first = jnp.concatenate([arrived[s] for s in members], axis=0)
        two = jnp.concatenate([first, swap(first, 1, 2)], axis=0)
        four = jnp.concatenate([two, swap(two, 2, 1)], axis=0)
        sources = me ^ (4 * jnp.array(members, jnp.int32)[None, :]) ^ near[:, None]
        kinds = kind_of[sources.reshape(-1)]
        keep, send = expert_call(
            kinds, four, pick, own_gu, other_gu, w_down, other_down, block_rows
        )
        keep = keep + swap(send, 2, 1).astype(jnp.float32)
        cut = first.shape[0]
        back = swap(keep[cut:].astype(jnp.bfloat16), 1, 2)
        keep = keep[:cut] + back.astype(jnp.float32)
        for i, s in enumerate(members):
            returned[s] = keep[i * block_rows : (i + 1) * block_rows]
    mixture = returned[0]
    for s in range(1, slots):
        mixture = mixture + swap(returned[s].astype(jnp.bfloat16), 4 * s, 4 * s).astype(jnp.float32)
    mine = payload[:, :model_width].astype(jnp.float32) + mixture
    theirs = swap_half(mine)
    hidden_out = jnp.where(
        core == 0,
        jnp.concatenate([mine, theirs], axis=0),
        jnp.concatenate([theirs, mine], axis=0),
    )

    normed = rms_scale(hidden_out, norm_gain).astype(jnp.bfloat16)
    head_dim = q_gain.shape[0]
    kv_width = key_value_weight.shape[2]
    kv_heads = kv_width // head_dim
    key_value = jnp.dot(
        normed,
        key_value_weight.reshape(model_width, 2 * kv_width),
        preferred_element_type=jnp.float32,
    )
    keys = rms_scale(key_value[:, :kv_width].reshape(tok_rows, kv_heads, head_dim), k_gain)
    own_kv = jnp.concatenate(
        [keys.reshape(tok_rows, kv_width), key_value[:, kv_width:]], axis=1
    ).astype(jnp.bfloat16)
    queries = jnp.dot(normed, w_query, preferred_element_type=jnp.float32)
    heads = queries.shape[1] // head_dim
    queries = rms_scale(queries.reshape(tok_rows, heads, head_dim), q_gain)
    queries = queries.reshape(tok_rows, heads * head_dim).astype(jnp.bfloat16)

    arrived = {0: own_kv}
    for s in range(1, slots):
        arrived[s] = swap(own_kv, 4 * s, 4 * s)
    kv_parts = []
    for members in slot_groups:
        first = jnp.concatenate([arrived[s] for s in members], axis=0)
        two = jnp.concatenate([first, swap(first, 1, 2)], axis=0)
        kv_parts += [two, swap(two, 2, 1)]
    attended = attention_call(queries, kv_parts, head_dim, heads // kv_heads)
    return hidden_out, attended


def solution(mesh):
    in_specs = (
        P("expert", None),
        P(),
        P("expert", None),
        P("expert", None),
        P("expert", None, None, "half"),
        P("expert", "half", None),
        P(),
        P(None, "half"),
        P(None, None, "half"),
        P(),
        P(),
    )
    out_specs = (P("expert", None), P("expert", "half"))
    return jax.shard_map(body, mesh=mesh, in_specs=in_specs, out_specs=out_specs, check_vma=False)
```

```python
import functools

import jax
import jax.numpy as jnp
from jax import lax
from jax.experimental import pallas as pl
from jax.experimental.pallas import tpu as pltpu
from jax.sharding import PartitionSpec as P

EPSILON = 1e-06
LANES = 128
KEYS_AT_ONCE = 2048
MIB = 1024 * 1024


def rms_scale(values, gain_row):
    mean_sq = jnp.mean(values * values, axis=-1, keepdims=True)
    return values * lax.rsqrt(mean_sq + EPSILON) * gain_row


def swap(value, mask_first, mask_second):
    pairs = []
    for expert in range(lax.axis_size("expert")):
        for half, mask in enumerate((mask_first, mask_second)):
            pairs.append((2 * expert + half, 2 * (expert ^ mask) + half))
    return lax.ppermute(value, ("expert", "half"), pairs)


def after(value, earlier):
    return lax.optimization_barrier((value, earlier))[0]


def swap_half(value):
    return lax.ppermute(value, "half", [(0, 1), (1, 0)])


def payload_kernel(groups, core_ref, hidden_ref, ids_ref, weights_ref, out_ref, table_ref):
    rows, width = hidden_ref.shape
    tokens = ids_ref.shape[1]
    row = lax.broadcasted_iota(jnp.int32, (LANES, tokens), 0)
    expert = jnp.where(row < groups, row, row - groups)
    table = jnp.zeros((LANES, tokens), jnp.float32)
    for j in range(ids_ref.shape[0]):
        table += jnp.where(ids_ref[j : j + 1] == expert, weights_ref[j : j + 1], 0.0)
    high = table.astype(jnp.bfloat16).astype(jnp.float32)
    extra = jnp.where(row < groups, high, jnp.where(row < 2 * groups, table - high, 0.0))
    table_ref[...] = extra.T
    mine = pl.ds(pl.multiple_of(core_ref[0] * rows, rows), rows)
    out_ref[:, :width] = hidden_ref[...]
    out_ref[:, width:] = table_ref[mine].astype(jnp.bfloat16)


def payload_call(core, hidden_in, expert_ids, route_weights, groups):
    tok_rows, width = hidden_in.shape
    rows = tok_rows // 2
    top = expert_ids.shape[1]
    return pl.pallas_call(
        functools.partial(payload_kernel, groups),
        out_shape=jax.ShapeDtypeStruct((rows, width + LANES), jnp.bfloat16),
        grid_spec=pltpu.PrefetchScalarGridSpec(
            num_scalar_prefetch=1,
            grid=(1,),
            in_specs=[
                pl.BlockSpec((rows, width), lambda i, core: (core[0], 0)),
                pl.BlockSpec((top, tok_rows), lambda i, core: (0, 0)),
                pl.BlockSpec((top, tok_rows), lambda i, core: (0, 0)),
            ],
            out_specs=pl.BlockSpec((rows, width + LANES), lambda i, core: (0, 0)),
            scratch_shapes=[pltpu.VMEM((tok_rows, LANES), jnp.float32)],
        ),
        name="payload",
    )(core, hidden_in, expert_ids.T, route_weights.T)


def expert_kernel(slots, units, place_ref, kind_ref, pick_ref, *refs):
    count = len(slots)
    x_refs, refs = refs[: 2 * count], refs[2 * count :]
    own_gu, other_gu, own_down, other_down = refs[:4]
    out_refs, refs = refs[4 : 4 + 2 * len(units)], refs[4 + 2 * len(units) :]
    gu_ref, down_ref, sorted_ref, act_ref, done_ref, sems = refs
    hidden_units, width = own_down.shape[1:]
    rows = x_refs[0].shape[0] // 2
    me, core = place_ref[0], place_ref[1]

    near = (0, 1 + core, 2 - core, 3)
    blocks = [(i, p) for i in range(count) for p in range(4)]
    kinds = [kind_ref[me ^ (4 * slots[i]) ^ near[p]] for i, p in blocks]
    images = functools.reduce(lambda a, b: a + b, kinds)
    first = (2 * images > len(blocks)).astype(jnp.int32)
    first_count = jnp.where(first == 1, images, len(blocks) - images)
    second_count = len(blocks) - first_count

    def copies(buffer, kind):
        found = []
        for k, gu in enumerate((own_gu, other_gu)):
            for c in range(2):
                at = pl.ds(c * hidden_units, hidden_units)
                found.append((gu.at[kind, c], gu_ref.at[buffer, k, :, at], sems.at[buffer, k, c]))
        for k, down in enumerate((own_down, other_down)):
            at = pl.ds(k * hidden_units, hidden_units)
            found.append((down.at[kind], down_ref.at[buffer, at], sems.at[buffer, k, 2]))
        return [pltpu.make_async_copy(*parts) for parts in found]

    for copy in copies(0, first):
        copy.start()

    @pl.when(second_count > 0)
    def _():
        for copy in copies(1, 1 - first):
            copy.start()

    offsets = []
    seen_first, seen_second = 0, first_count
    for kind in kinds:
        is_first = (kind == first).astype(jnp.int32)
        offsets.append(pl.multiple_of(jnp.where(is_first == 1, seen_first, seen_second) * rows, rows))
        seen_first, seen_second = seen_first + is_first, seen_second + 1 - is_first
    for (i, p), offset in zip(blocks, offsets):
        source = x_refs[2 * i + p // 2]
        sorted_ref[pl.ds(offset, rows)] = source[(p % 2) * rows : (p % 2 + 1) * rows]

    def rows_of(block, number):
        return pl.ds(pl.multiple_of(block * rows, rows), number * rows)

    def activate(buffer, k, block, number):
        at = rows_of(block, number)
        pre = jnp.dot(sorted_ref[at, :width], gu_ref[buffer, k], preferred_element_type=jnp.float32)
        gate, up = pre[:, :hidden_units], pre[:, hidden_units:]
        act = gate / (1.0 + jnp.exp(-gate)) * up
        act_ref[at, k * hidden_units : (k + 1) * hidden_units] = act.astype(jnp.bfloat16)

    def finish(buffer, block, number):
        at = rows_of(block, number)
        extra = sorted_ref[at, width:].astype(jnp.float32)
        weight = jnp.sum(extra * pick_ref[...], axis=-1, keepdims=True)
        out = jnp.dot(act_ref[at], down_ref[buffer], preferred_element_type=jnp.float32)
        done_ref[at] = out.astype(jnp.bfloat16).astype(jnp.float32) * weight

    def over_blocks(step, start, number):
        rest = lax.rem(number, 4)
        wholes = number // 4 + (rest == 3).astype(jnp.int32)

        def whole(at, carry):
            step(start + 4 * at, 4)
            return carry

        lax.fori_loop(0, wholes, whole, 0)

        @pl.when((rest == 1) | (rest == 2))
        def _():
            step(start + 4 * wholes, 2)

    def expert(buffer, kind, start, number):
        found = copies(buffer, kind)
        for k in range(2):
            for copy in found[2 * k : 2 * k + 2]:
                copy.wait()
            over_blocks(functools.partial(activate, buffer, k), start, number)
        for copy in found[4:]:
            copy.wait()
        over_blocks(functools.partial(finish, buffer), start, number)

    expert(0, first, 0, first_count)

    @pl.when(second_count > 0)
    def _():
        expert(1, 1 - first, first_count, second_count)

    for (i, p), offset in zip(blocks, offsets):
        for u, unit in enumerate(units):
            if slots[i] in unit:
                row = ((p % 2) * len(unit) + unit.index(slots[i])) * rows
                target = out_refs[2 * u + p // 2]
                target[row : row + rows] = done_ref[pl.ds(offset, rows)].astype(target.dtype)


def expert_call(slots, units, place, kinds, pick, parts, weights):
    rows = parts[0].shape[0] // 2
    _, hidden_units, width = weights[2].shape
    vmem, anywhere = pl.BlockSpec(memory_space=pltpu.VMEM), pl.BlockSpec(memory_space=pl.ANY)
    smem = pl.BlockSpec(memory_space=pltpu.SMEM)
    room = (4 * len(slots) + 4) * rows
    shapes = []
    for unit in units:
        for dtype in (jnp.float32, jnp.bfloat16):
            shapes.append(jax.ShapeDtypeStruct((2 * len(unit) * rows, width), dtype))
    return pl.pallas_call(
        functools.partial(expert_kernel, slots, units),
        out_shape=tuple(shapes),
        in_specs=[smem, smem, vmem] + [vmem] * len(parts) + [anywhere] * 4,
        out_specs=(vmem,) * len(shapes),
        scratch_shapes=[
            pltpu.VMEM((2, 2, width, 2 * hidden_units), jnp.bfloat16),
            pltpu.VMEM((2, 2 * hidden_units, width), jnp.bfloat16),
            pltpu.VMEM((room, width + LANES), jnp.bfloat16),
            pltpu.VMEM((room, 2 * hidden_units), jnp.bfloat16),
            pltpu.VMEM((room, width), jnp.float32),
            pltpu.SemaphoreType.DMA((2, 2, 3)),
        ],
        compiler_params=pltpu.CompilerParams(vmem_limit_bytes=36 * MIB),
        name="experts",
    )(place, kinds, pick, *parts, *weights)


def attention_kernel(head_dim, group, q_ref, *refs):
    kv_refs, out_ref = refs[:-1], refs[-1]
    kv_heads = kv_refs[0].shape[1] // (2 * head_dim)
    scale = head_dim**-0.5
    rows = q_ref.shape[0]
    step = max(1, KEYS_AT_ONCE // kv_refs[0].shape[0])
    def columns(ref, head, count=1):
        return ref[:, pl.ds(pl.multiple_of(head * head_dim, head_dim), count * head_dim)]

    def two_heads(pair, carry):
        g = pair // (group // 2)
        both = columns(q_ref, 2 * pair, 2)
        q = jnp.concatenate([both[:, :head_dim], both[:, head_dim:]], axis=0)
        keys = [columns(ref, g) for ref in kv_refs]
        vals = [columns(ref, kv_heads + g) for ref in kv_refs]
        peak, total, mixed = None, 0.0, 0.0
        for at in range(0, len(keys), step):
            scores = [
                lax.dot_general(q, k, (((1,), (1,)), ((), ())), preferred_element_type=jnp.float32)
                for k in keys[at : at + step]
            ]
            peaks = [jnp.max(s, axis=-1, keepdims=True) for s in scores]
            if peak is not None:
                before = peak
                peak = functools.reduce(jnp.maximum, peaks + [before])
                shrink = jnp.exp((before - peak) * scale)
                total, mixed = total * shrink, mixed * shrink
            else:
                peak = functools.reduce(jnp.maximum, peaks)
            for s, v in zip(scores, vals[at : at + step]):
                p = jnp.exp((s - peak) * scale)
                total = total + jnp.sum(p, axis=-1, keepdims=True)
                mixed = mixed + jnp.dot(
                    p.astype(jnp.bfloat16), v, preferred_element_type=jnp.float32
                )
        mixed = (mixed / total).astype(jnp.bfloat16)
        at = pl.multiple_of(2 * pair * head_dim, 2 * head_dim)
        out_ref[:, pl.ds(at, 2 * head_dim)] = jnp.concatenate([mixed[:rows], mixed[rows:]], axis=1)
        return carry

    lax.fori_loop(0, kv_heads * group // 2, two_heads, 0, unroll=2 if len(kv_refs) <= 8 and step >= len(kv_refs) else 1)


def attention_call(queries, kv_parts, head_dim, group):
    vmem = pl.BlockSpec(memory_space=pltpu.VMEM)
    rows, width = queries.shape
    keys = sum(part.shape[0] for part in kv_parts)
    return pl.pallas_call(
        functools.partial(attention_kernel, head_dim, group),
        out_shape=jax.ShapeDtypeStruct((rows, width), jnp.bfloat16),
        in_specs=[vmem] * (1 + len(kv_parts)),
        out_specs=vmem,
        compiler_params=pltpu.CompilerParams(vmem_limit_bytes=48 * MIB),
        name="attention",
    )(queries, *kv_parts)


def body(
    hidden_in,
    modality,
    expert_ids,
    route_weights,
    w_gate_up,
    w_down,
    norm_gain,
    w_query,
    key_value_weight,
    q_gain,
    k_gain,
):
    tok_rows, model_width = hidden_in.shape
    groups = lax.axis_size("expert")
    me, core = lax.axis_index("expert"), lax.axis_index("half")
    slots = groups // 4
    slot_order = [0] + list(range(2, slots, 2)) + list(range(1, slots, 2))
    slot_groups = [[s, s + 2] for s in range(0, slots, 4)] + [[s, s + 2] for s in range(1, slots, 4)]

    payload = payload_call(core[None], hidden_in, expert_ids, route_weights, groups)
    lane = jnp.arange(LANES, dtype=jnp.int32)
    pick = ((lane == me) | (lane == me + groups)).astype(jnp.float32)[None, :]
    kinds = modality.reshape(groups, tok_rows)[:, 0]
    place = jnp.stack([me, core]).astype(jnp.int32)

    arrived = {0: payload}
    for s in range(1, slots):
        arrived[s] = swap(payload, 4 * s, 4 * s)
    own_gu = w_gate_up.transpose(0, 2, 1, 3)
    weights = (own_gu, swap_half(own_gu), w_down, swap_half(w_down))

    jobs = []

    def cross(value, *masks):
        if len(jobs) > 1:
            value = after(value, jobs[-2])
        jobs.append(swap(value, *masks))
        return jobs[-1]

    two, four, outs, returned = {}, {}, {}, {}

    def collect(members, last):
        for s in members:
            two[s] = jnp.concatenate([arrived[s], cross(arrived[s], 1, 2)], axis=0)
            if last is not None and s == members[-1]:
                two[s] = after(two[s], last)
            four[s] = cross(two[s], 2, 1)

    def work(members):
        units = [[s] for s in reversed(members)]
        parts = [part for s in members for part in (two[s], four[s])]
        found = expert_call(members, units, place, kinds, pick, parts, weights)
        for u, unit in enumerate(units):
            outs[unit[0]] = found[2 * u : 2 * u + 2]
        return found[0]

    def give_back(members):
        for s in reversed(members):
            keep, send = outs[s]
            keep = keep + swap(send, 2, 1).astype(jnp.float32)
            cut = keep.shape[0] // 2
            back = swap(keep[cut:].astype(jnp.bfloat16), 1, 2)
            returned[s] = keep[:cut] + back.astype(jnp.float32)

    collect(slot_groups[0], None)
    for before, members in zip(slot_groups, slot_groups[1:]):
        collect(members, work(before))
        give_back(before)
    work(slot_groups[-1])
    give_back(slot_groups[-1])
    mixture = returned[0]
    for s in range(1, slots):
        mixture = mixture + swap(returned[s].astype(jnp.bfloat16), 4 * s, 4 * s).astype(jnp.float32)
    mine = payload[:, :model_width].astype(jnp.float32) + mixture
    theirs = swap_half(mine)
    hidden_out = jnp.where(
        core == 0,
        jnp.concatenate([mine, theirs], axis=0),
        jnp.concatenate([theirs, mine], axis=0),
    )

    normed = rms_scale(hidden_out, norm_gain).astype(jnp.bfloat16)
    head_dim = q_gain.shape[0]
    kv_width = key_value_weight.shape[2]
    kv_heads = kv_width // head_dim
    key_value = jnp.dot(
        normed,
        key_value_weight.reshape(model_width, 2 * kv_width),
        preferred_element_type=jnp.float32,
    )
    keys = rms_scale(key_value[:, :kv_width].reshape(tok_rows, kv_heads, head_dim), k_gain)
    own_kv = jnp.concatenate(
        [keys.reshape(tok_rows, kv_width), key_value[:, kv_width:]], axis=1
    ).astype(jnp.bfloat16)
    queries = jnp.dot(normed, w_query, preferred_element_type=jnp.float32)
    heads = queries.shape[1] // head_dim
    queries = rms_scale(queries.reshape(tok_rows, heads, head_dim), q_gain)
    queries = queries.reshape(tok_rows, heads * head_dim).astype(jnp.bfloat16)

    arrived = {0: own_kv}
    for s in range(1, slots):
        arrived[s] = swap(own_kv, 4 * s, 4 * s)
    kv_parts = []
    for s in slot_order:
        pair = jnp.concatenate([arrived[s], swap(arrived[s], 1, 2)], axis=0)
        kv_parts += [pair, swap(pair, 2, 1)]
    attended = attention_call(queries, kv_parts, head_dim, heads // kv_heads)
    return hidden_out, attended


def solution(mesh):
    in_specs = (
        P("expert", None),
        P(),
        P("expert", None),
        P("expert", None),
        P("expert", None, None, "half"),
        P("expert", "half", None),
        P(),
        P(None, "half"),
        P(None, None, "half"),
        P(),
        P(),
    )
    out_specs = (P("expert", None), P("expert", "half"))
    return jax.shard_map(body, mesh=mesh, in_specs=in_specs, out_specs=out_specs, check_vma=False)
```

```python
import functools

import jax
import jax.numpy as jnp
from jax import lax
from jax.experimental import pallas as pl
from jax.experimental.pallas import tpu as pltpu
from jax.sharding import PartitionSpec as P

EPSILON = 1e-06
LANES = 128
KEYS_AT_ONCE = 2048
LOG2_E = 1.4426950408889634
MIB = 1024 * 1024


def rms_scale(values, gain_row):
    mean_sq = jnp.mean(values * values, axis=-1, keepdims=True)
    return values * lax.rsqrt(mean_sq + EPSILON) * gain_row


def swap(value, mask_first, mask_second):
    pairs = []
    for expert in range(lax.axis_size("expert")):
        for half, mask in enumerate((mask_first, mask_second)):
            pairs.append((2 * expert + half, 2 * (expert ^ mask) + half))
    return lax.ppermute(value, ("expert", "half"), pairs)


def after(value, earlier):
    return lax.optimization_barrier((value, earlier))[0]


def swap_half(value):
    return lax.ppermute(value, "half", [(0, 1), (1, 0)])


def payload_kernel(groups, core_ref, hidden_ref, ids_ref, weights_ref, out_ref, table_ref):
    rows, width = hidden_ref.shape
    tokens = ids_ref.shape[1]
    row = lax.broadcasted_iota(jnp.int32, (LANES, tokens), 0)
    expert = jnp.where(row < groups, row, row - groups)
    table = jnp.zeros((LANES, tokens), jnp.float32)
    for j in range(ids_ref.shape[0]):
        table += jnp.where(ids_ref[j : j + 1] == expert, weights_ref[j : j + 1], 0.0)
    high = table.astype(jnp.bfloat16).astype(jnp.float32)
    extra = jnp.where(row < groups, high, jnp.where(row < 2 * groups, table - high, 0.0))
    table_ref[...] = extra.T
    mine = pl.ds(pl.multiple_of(core_ref[0] * rows, rows), rows)
    out_ref[:, :width] = hidden_ref[...]
    out_ref[:, width:] = table_ref[mine].astype(jnp.bfloat16)


def payload_call(core, hidden_in, expert_ids, route_weights, groups):
    tok_rows, width = hidden_in.shape
    rows = tok_rows // 2
    top = expert_ids.shape[1]
    return pl.pallas_call(
        functools.partial(payload_kernel, groups),
        out_shape=jax.ShapeDtypeStruct((rows, width + LANES), jnp.bfloat16),
        grid_spec=pltpu.PrefetchScalarGridSpec(
            num_scalar_prefetch=1,
            grid=(1,),
            in_specs=[
                pl.BlockSpec((rows, width), lambda i, core: (core[0], 0)),
                pl.BlockSpec((top, tok_rows), lambda i, core: (0, 0)),
                pl.BlockSpec((top, tok_rows), lambda i, core: (0, 0)),
            ],
            out_specs=pl.BlockSpec((rows, width + LANES), lambda i, core: (0, 0)),
            scratch_shapes=[pltpu.VMEM((tok_rows, LANES), jnp.float32)],
        ),
        name="payload",
    )(core, hidden_in, expert_ids.T, route_weights.T)


def expert_kernel(slots, units, place_ref, kind_ref, pick_ref, *refs):
    count = len(slots)
    x_refs, refs = refs[: 2 * count], refs[2 * count :]
    own_gu, other_gu, own_down, other_down = refs[:4]
    out_refs, refs = refs[4 : 4 + 2 * len(units)], refs[4 + 2 * len(units) :]
    gu_ref, down_ref, sorted_ref, act_ref, done_ref, sems = refs
    hidden_units, width = own_down.shape[1:]
    rows = x_refs[0].shape[0] // 2
    me, core = place_ref[0], place_ref[1]

    near = (0, 1 + core, 2 - core, 3)
    blocks = [(i, p) for i in range(count) for p in range(4)]
    kinds = [kind_ref[me ^ (4 * slots[i]) ^ near[p]] for i, p in blocks]
    images = functools.reduce(lambda a, b: a + b, kinds)
    first = (2 * images > len(blocks)).astype(jnp.int32)
    first_count = jnp.where(first == 1, images, len(blocks) - images)
    second_count = len(blocks) - first_count

    def copies(buffer, kind):
        found = []
        for k, gu in enumerate((own_gu, other_gu)):
            for c in range(2):
                at = pl.ds(c * hidden_units, hidden_units)
                found.append((gu.at[kind, c], gu_ref.at[buffer, k, :, at], sems.at[buffer, k, c]))
        for k, down in enumerate((own_down, other_down)):
            at = pl.ds(k * hidden_units, hidden_units)
            found.append((down.at[kind], down_ref.at[buffer, at], sems.at[buffer, k, 2]))
        return [pltpu.make_async_copy(*parts) for parts in found]

    for copy in copies(0, first):
        copy.start()

    @pl.when(second_count > 0)
    def _():
        for copy in copies(1, 1 - first):
            copy.start()

    offsets = []
    seen_first, seen_second = 0, first_count
    for kind in kinds:
        is_first = (kind == first).astype(jnp.int32)
        offsets.append(pl.multiple_of(jnp.where(is_first == 1, seen_first, seen_second) * rows, rows))
        seen_first, seen_second = seen_first + is_first, seen_second + 1 - is_first
    for (i, p), offset in zip(blocks, offsets):
        source = x_refs[2 * i + p // 2]
        sorted_ref[pl.ds(offset, rows)] = source[(p % 2) * rows : (p % 2 + 1) * rows]

    def rows_of(block, number):
        return pl.ds(pl.multiple_of(block * rows, rows), number * rows)

    def activate(buffer, k, block, number):
        at = rows_of(block, number)
        pre = jnp.dot(sorted_ref[at, :width], gu_ref[buffer, k], preferred_element_type=jnp.float32)
        gate, up = pre[:, :hidden_units], pre[:, hidden_units:]
        act = gate / (1.0 + jnp.exp(-gate)) * up
        act_ref[at, k * hidden_units : (k + 1) * hidden_units] = act.astype(jnp.bfloat16)

    def finish(buffer, block, number):
        at = rows_of(block, number)
        extra = sorted_ref[at, width:].astype(jnp.float32)
        weight = jnp.sum(extra * pick_ref[...], axis=-1, keepdims=True)
        out = jnp.dot(act_ref[at], down_ref[buffer], preferred_element_type=jnp.float32)
        done_ref[at] = out.astype(jnp.bfloat16).astype(jnp.float32) * weight

    def over_blocks(step, start, number):
        rest = lax.rem(number, 4)
        wholes = number // 4 + (rest == 3).astype(jnp.int32)

        def whole(at, carry):
            step(start + 4 * at, 4)
            return carry

        lax.fori_loop(0, wholes, whole, 0)

        @pl.when((rest == 1) | (rest == 2))
        def _():
            step(start + 4 * wholes, 2)

    def expert(buffer, kind, start, number):
        found = copies(buffer, kind)
        for k in range(2):
            for copy in found[2 * k : 2 * k + 2]:
                copy.wait()
            over_blocks(functools.partial(activate, buffer, k), start, number)
        for copy in found[4:]:
            copy.wait()
        over_blocks(functools.partial(finish, buffer), start, number)

    expert(0, first, 0, first_count)

    @pl.when(second_count > 0)
    def _():
        expert(1, 1 - first, first_count, second_count)

    for (i, p), offset in zip(blocks, offsets):
        for u, unit in enumerate(units):
            if slots[i] in unit:
                row = ((p % 2) * len(unit) + unit.index(slots[i])) * rows
                target = out_refs[2 * u + p // 2]
                target[row : row + rows] = done_ref[pl.ds(offset, rows)].astype(target.dtype)


def expert_call(slots, units, place, kinds, pick, parts, weights):
    rows = parts[0].shape[0] // 2
    _, hidden_units, width = weights[2].shape
    vmem, anywhere = pl.BlockSpec(memory_space=pltpu.VMEM), pl.BlockSpec(memory_space=pl.ANY)
    smem = pl.BlockSpec(memory_space=pltpu.SMEM)
    room = (4 * len(slots) + 4) * rows
    shapes = []
    for unit in units:
        for dtype in (jnp.float32, jnp.bfloat16):
            shapes.append(jax.ShapeDtypeStruct((2 * len(unit) * rows, width), dtype))
    return pl.pallas_call(
        functools.partial(expert_kernel, slots, units),
        out_shape=tuple(shapes),
        in_specs=[smem, smem, vmem] + [vmem] * len(parts) + [anywhere] * 4,
        out_specs=(vmem,) * len(shapes),
        scratch_shapes=[
            pltpu.VMEM((2, 2, width, 2 * hidden_units), jnp.bfloat16),
            pltpu.VMEM((2, 2 * hidden_units, width), jnp.bfloat16),
            pltpu.VMEM((room, width + LANES), jnp.bfloat16),
            pltpu.VMEM((room, 2 * hidden_units), jnp.bfloat16),
            pltpu.VMEM((room, width), jnp.float32),
            pltpu.SemaphoreType.DMA((2, 2, 3)),
        ],
        compiler_params=pltpu.CompilerParams(vmem_limit_bytes=36 * MIB),
        name="experts",
    )(place, kinds, pick, *parts, *weights)


def attention_kernel(head_dim, group, kv_count, resumes, ends, q_ref, *refs):
    kv_refs, refs = refs[:kv_count], refs[kv_count:]
    if resumes:
        stats_in, mixed_in, refs = refs[0], refs[1], refs[2:]
    rows = q_ref.shape[0]
    kv_heads = kv_refs[0].shape[1] // (2 * head_dim)
    step = max(1, KEYS_AT_ONCE // kv_refs[0].shape[0])
    scale = head_dim**-0.5 * LOG2_E

    def columns(ref, head, count=1):
        return ref[:, pl.ds(pl.multiple_of(head * head_dim, head_dim), count * head_dim)]

    def one_group(g, carry):
        wide = columns(q_ref, group * g, group)
        q = jnp.concatenate(
            [wide[:, i * head_dim : (i + 1) * head_dim] for i in range(group)], axis=0
        )
        peak, total, mixed = None, 0.0, 0.0
        if resumes:
            peak, total, mixed = stats_in[g, 0:1], stats_in[g, 1:2], mixed_in[g]
        for at in range(0, kv_count, step):
            scores = [
                lax.dot_general(
                    columns(ref, g), q, (((1,), (1,)), ((), ())), preferred_element_type=jnp.float32
                )
                for ref in kv_refs[at : at + step]
            ]
            peaks = [jnp.max(s, axis=0, keepdims=True) for s in scores]
            if peak is not None:
                before = peak
                peak = functools.reduce(jnp.maximum, peaks + [before])
                shrink = jnp.exp2((before - peak) * scale)
                total, mixed = total * shrink, mixed * shrink
            else:
                peak = functools.reduce(jnp.maximum, peaks)
            for s, ref in zip(scores, kv_refs[at : at + step]):
                p = jnp.exp2((s - peak) * scale)
                total = total + jnp.sum(p, axis=0, keepdims=True)
                mixed = mixed + lax.dot_general(
                    columns(ref, kv_heads + g),
                    p.astype(jnp.bfloat16),
                    (((0,), (0,)), ((), ())),
                    preferred_element_type=jnp.float32,
                )
        if ends:
            out = (mixed / total).T.astype(jnp.bfloat16)
            at = pl.multiple_of(group * g * head_dim, group * head_dim)
            refs[0][:, pl.ds(at, group * head_dim)] = jnp.concatenate(
                [out[i * rows : (i + 1) * rows] for i in range(group)], axis=1
            )
        else:
            refs[0][g, 0:1] = peak
            refs[0][g, 1:2] = total
            refs[1][g] = mixed
        return carry

    lax.fori_loop(0, kv_heads, one_group, 0, unroll=kv_heads if kv_count <= step else 1)


def attention_call(queries, kv_parts, head_dim, group, state, ends):
    vmem = pl.BlockSpec(memory_space=pltpu.VMEM)
    rows, width = queries.shape
    keys = sum(part.shape[0] for part in kv_parts)
    kv_heads = width // (head_dim * group)
    shapes = (jax.ShapeDtypeStruct((rows, width), jnp.bfloat16),)
    if not ends:
        shapes = (
            jax.ShapeDtypeStruct((kv_heads, 8, group * rows), jnp.float32),
            jax.ShapeDtypeStruct((kv_heads, head_dim, group * rows), jnp.float32),
        )
    state = state or ()
    return pl.pallas_call(
        functools.partial(attention_kernel, head_dim, group, len(kv_parts), bool(state), ends),
        out_shape=shapes,
        in_specs=[vmem] * (1 + len(kv_parts) + len(state)),
        out_specs=(vmem,) * len(shapes),
        compiler_params=pltpu.CompilerParams(vmem_limit_bytes=48 * MIB),
        cost_estimate=pl.CostEstimate(
            flops=4 * rows * keys * width,
            bytes_accessed=4 * rows * width,
            transcendentals=rows * keys * width // head_dim,
        ),
        name="attention",
    )(queries, *kv_parts, *state)


def body(
    hidden_in,
    modality,
    expert_ids,
    route_weights,
    w_gate_up,
    w_down,
    norm_gain,
    w_query,
    key_value_weight,
    q_gain,
    k_gain,
):
    tok_rows, model_width = hidden_in.shape
    groups = lax.axis_size("expert")
    me, core = lax.axis_index("expert"), lax.axis_index("half")
    slots = groups // 4
    slot_order = [0] + list(range(2, slots, 2)) + list(range(1, slots, 2))
    slot_groups = [[s, s + 2] for s in range(0, slots, 4)] + [[s, s + 2] for s in range(1, slots, 4)]

    payload = payload_call(core[None], hidden_in, expert_ids, route_weights, groups)
    lane = jnp.arange(LANES, dtype=jnp.int32)
    pick = ((lane == me) | (lane == me + groups)).astype(jnp.float32)[None, :]
    kinds = modality.reshape(groups, tok_rows)[:, 0]
    place = jnp.stack([me, core]).astype(jnp.int32)

    arrived = {0: payload}
    for s in range(1, slots):
        arrived[s] = swap(payload, 4 * s, 4 * s)
    own_gu = w_gate_up.transpose(0, 2, 1, 3)
    weights = (own_gu, swap_half(own_gu), w_down, swap_half(w_down))

    jobs = []

    def cross(value, *masks):
        if len(jobs) > 1:
            value = after(value, jobs[-2])
        jobs.append(swap(value, *masks))
        return jobs[-1]

    two, four, outs, returned = {}, {}, {}, {}

    def collect(members, last):
        for s in members:
            two[s] = jnp.concatenate([arrived[s], cross(arrived[s], 1, 2)], axis=0)
            if last is not None and s == members[-1]:
                two[s] = after(two[s], last)
            four[s] = cross(two[s], 2, 1)

    def work(members):
        units = [[s] for s in reversed(members)]
        parts = [part for s in members for part in (two[s], four[s])]
        found = expert_call(members, units, place, kinds, pick, parts, weights)
        for u, unit in enumerate(units):
            outs[unit[0]] = found[2 * u : 2 * u + 2]
        return found[0]

    def give_back(members):
        for s in reversed(members):
            keep, send = outs[s]
            keep = keep + swap(send, 2, 1).astype(jnp.float32)
            cut = keep.shape[0] // 2
            back = swap(keep[cut:].astype(jnp.bfloat16), 1, 2)
            returned[s] = keep[:cut] + back.astype(jnp.float32)

    collect(slot_groups[0], None)
    for before, members in zip(slot_groups, slot_groups[1:]):
        collect(members, work(before))
        give_back(before)
    work(slot_groups[-1])
    give_back(slot_groups[-1])
    mixture = returned[0]
    for s in range(1, slots):
        mixture = mixture + swap(returned[s].astype(jnp.bfloat16), 4 * s, 4 * s).astype(jnp.float32)
    mine = payload[:, :model_width].astype(jnp.float32) + mixture
    theirs = swap_half(mine)
    hidden_out = jnp.where(
        core == 0,
        jnp.concatenate([mine, theirs], axis=0),
        jnp.concatenate([theirs, mine], axis=0),
    )

    normed = rms_scale(hidden_out, norm_gain).astype(jnp.bfloat16)
    head_dim = q_gain.shape[0]
    kv_width = key_value_weight.shape[2]
    kv_heads = kv_width // head_dim
    key_value = jnp.dot(
        normed,
        key_value_weight.reshape(model_width, 2 * kv_width),
        preferred_element_type=jnp.float32,
    )
    keys = rms_scale(key_value[:, :kv_width].reshape(tok_rows, kv_heads, head_dim), k_gain)
    own_kv = jnp.concatenate(
        [keys.reshape(tok_rows, kv_width), key_value[:, kv_width:]], axis=1
    ).astype(jnp.bfloat16)
    queries = jnp.dot(normed, w_query, preferred_element_type=jnp.float32)
    heads = queries.shape[1] // head_dim
    queries = rms_scale(queries.reshape(tok_rows, heads, head_dim), q_gain)
    queries = queries.reshape(tok_rows, heads * head_dim).astype(jnp.bfloat16)

    arrived = {0: own_kv}
    for s in range(1, slots):
        arrived[s] = swap(own_kv, 4 * s, 4 * s)
    kv_parts = []
    for s in slot_order:
        pair = jnp.concatenate([arrived[s], swap(arrived[s], 1, 2)], axis=0)
        kv_parts += [pair, swap(pair, 2, 1)]
    state = attention_call(queries, kv_parts[:-4], head_dim, heads // kv_heads, None, False)
    (attended,) = attention_call(queries, kv_parts[-4:], head_dim, heads // kv_heads, state, True)
    return hidden_out, attended


def solution(mesh):
    in_specs = (
        P("expert", None),
        P(),
        P("expert", None),
        P("expert", None),
        P("expert", None, None, "half"),
        P("expert", "half", None),
        P(),
        P(None, "half"),
        P(None, None, "half"),
        P(),
        P(),
    )
    out_specs = (P("expert", None), P("expert", "half"))
    return jax.shard_map(body, mesh=mesh, in_specs=in_specs, out_specs=out_specs, check_vma=False)
```

```python
import functools

import jax
import jax.numpy as jnp
from jax import lax
from jax.experimental import pallas as pl
from jax.experimental.pallas import tpu as pltpu
from jax.sharding import PartitionSpec as P

EPSILON = 1e-06
LANES = 128
KEYS_AT_ONCE = 2048
LOG2_E = 1.4426950408889634
MIB = 1024 * 1024


def rms_scale(values, gain_row):
    mean_sq = jnp.mean(values * values, axis=-1, keepdims=True)
    return values * lax.rsqrt(mean_sq + EPSILON) * gain_row


def swap(value, mask_first, mask_second):
    pairs = []
    for expert in range(lax.axis_size("expert")):
        for half, mask in enumerate((mask_first, mask_second)):
            pairs.append((2 * expert + half, 2 * (expert ^ mask) + half))
    return lax.ppermute(value, ("expert", "half"), pairs)


def after(value, earlier):
    return lax.optimization_barrier((value, earlier))[0]


def swap_half(value):
    return lax.ppermute(value, "half", [(0, 1), (1, 0)])


def payload_kernel(groups, core_ref, hidden_ref, ids_ref, weights_ref, out_ref, table_ref):
    rows, width = hidden_ref.shape
    tokens = ids_ref.shape[1]
    row = lax.broadcasted_iota(jnp.int32, (LANES, tokens), 0)
    expert = jnp.where(row < groups, row, row - groups)
    table = jnp.zeros((LANES, tokens), jnp.float32)
    for j in range(ids_ref.shape[0]):
        table += jnp.where(ids_ref[j : j + 1] == expert, weights_ref[j : j + 1], 0.0)
    high = table.astype(jnp.bfloat16).astype(jnp.float32)
    extra = jnp.where(row < groups, high, jnp.where(row < 2 * groups, table - high, 0.0))
    table_ref[...] = extra.T
    mine = pl.ds(pl.multiple_of(core_ref[0] * rows, rows), rows)
    out_ref[:, :width] = hidden_ref[...]
    out_ref[:, width:] = table_ref[mine].astype(jnp.bfloat16)


def payload_call(core, hidden_in, expert_ids, route_weights, groups):
    tok_rows, width = hidden_in.shape
    rows = tok_rows // 2
    top = expert_ids.shape[1]
    return pl.pallas_call(
        functools.partial(payload_kernel, groups),
        out_shape=jax.ShapeDtypeStruct((rows, width + LANES), jnp.bfloat16),
        grid_spec=pltpu.PrefetchScalarGridSpec(
            num_scalar_prefetch=1,
            grid=(1,),
            in_specs=[
                pl.BlockSpec((rows, width), lambda i, core: (core[0], 0)),
                pl.BlockSpec((top, tok_rows), lambda i, core: (0, 0)),
                pl.BlockSpec((top, tok_rows), lambda i, core: (0, 0)),
            ],
            out_specs=pl.BlockSpec((rows, width + LANES), lambda i, core: (0, 0)),
            scratch_shapes=[pltpu.VMEM((tok_rows, LANES), jnp.float32)],
        ),
        name="payload",
    )(core, hidden_in, expert_ids.T, route_weights.T)


def expert_kernel(slots, units, place_ref, kind_ref, pick_ref, *refs):
    count = len(slots)
    x_refs, refs = refs[: 2 * count], refs[2 * count :]
    own_gu, other_gu, own_down, other_down = refs[:4]
    out_refs, refs = refs[4 : 4 + 2 * len(units)], refs[4 + 2 * len(units) :]
    gu_ref, down_ref, sorted_ref, act_ref, done_ref, sems = refs
    hidden_units, width = own_down.shape[1:]
    rows = x_refs[0].shape[0] // 2
    me, core = place_ref[0], place_ref[1]

    near = (0, 1 + core, 2 - core, 3)
    blocks = [(i, p) for i in range(count) for p in range(4)]
    kinds = [kind_ref[me ^ (4 * slots[i]) ^ near[p]] for i, p in blocks]
    images = functools.reduce(lambda a, b: a + b, kinds)
    first = (2 * images > len(blocks)).astype(jnp.int32)
    first_count = jnp.where(first == 1, images, len(blocks) - images)
    second_count = len(blocks) - first_count

    def copies(buffer, kind):
        found = []
        for k, gu in enumerate((own_gu, other_gu)):
            for c in range(2):
                at = pl.ds(c * hidden_units, hidden_units)
                found.append((gu.at[kind, c], gu_ref.at[buffer, k, :, at], sems.at[buffer, k, c]))
        for k, down in enumerate((own_down, other_down)):
            at = pl.ds(k * hidden_units, hidden_units)
            found.append((down.at[kind], down_ref.at[buffer, at], sems.at[buffer, k, 2]))
        return [pltpu.make_async_copy(*parts) for parts in found]

    for copy in copies(0, first):
        copy.start()

    @pl.when(second_count > 0)
    def _():
        for copy in copies(1, 1 - first):
            copy.start()

    offsets = []
    seen_first, seen_second = 0, first_count
    for kind in kinds:
        is_first = (kind == first).astype(jnp.int32)
        offsets.append(pl.multiple_of(jnp.where(is_first == 1, seen_first, seen_second) * rows, rows))
        seen_first, seen_second = seen_first + is_first, seen_second + 1 - is_first
    for (i, p), offset in zip(blocks, offsets):
        source = x_refs[2 * i + p // 2]
        sorted_ref[pl.ds(offset, rows)] = source[(p % 2) * rows : (p % 2 + 1) * rows]

    def rows_of(block, number):
        return pl.ds(pl.multiple_of(block * rows, rows), number * rows)

    def activate(buffer, k, block, number):
        at = rows_of(block, number)
        pre = jnp.dot(sorted_ref[at, :width], gu_ref[buffer, k], preferred_element_type=jnp.float32)
        gate, up = pre[:, :hidden_units], pre[:, hidden_units:]
        act = gate / (1.0 + jnp.exp(-gate)) * up
        act_ref[at, k * hidden_units : (k + 1) * hidden_units] = act.astype(jnp.bfloat16)

    def finish(buffer, block, number):
        at = rows_of(block, number)
        extra = sorted_ref[at, width:].astype(jnp.float32)
        weight = jnp.sum(extra * pick_ref[...], axis=-1, keepdims=True)
        out = jnp.dot(act_ref[at], down_ref[buffer], preferred_element_type=jnp.float32)
        done_ref[at] = out.astype(jnp.bfloat16).astype(jnp.float32) * weight

    def over_blocks(step, start, number):
        rest = lax.rem(number, 4)
        wholes = number // 4 + (rest == 3).astype(jnp.int32)

        def whole(at, carry):
            step(start + 4 * at, 4)
            return carry

        lax.fori_loop(0, wholes, whole, 0)

        @pl.when((rest == 1) | (rest == 2))
        def _():
            step(start + 4 * wholes, 2)

    def expert(buffer, kind, start, number):
        found = copies(buffer, kind)
        for k in range(2):
            for copy in found[2 * k : 2 * k + 2]:
                copy.wait()
            over_blocks(functools.partial(activate, buffer, k), start, number)
        for copy in found[4:]:
            copy.wait()
        over_blocks(functools.partial(finish, buffer), start, number)

    expert(0, first, 0, first_count)

    @pl.when(second_count > 0)
    def _():
        expert(1, 1 - first, first_count, second_count)

    for (i, p), offset in zip(blocks, offsets):
        for u, unit in enumerate(units):
            if slots[i] in unit:
                row = ((p % 2) * len(unit) + unit.index(slots[i])) * rows
                target = out_refs[2 * u + p // 2]
                target[row : row + rows] = done_ref[pl.ds(offset, rows)].astype(target.dtype)


def expert_call(slots, units, place, kinds, pick, parts, weights):
    rows = parts[0].shape[0] // 2
    _, hidden_units, width = weights[2].shape
    vmem, anywhere = pl.BlockSpec(memory_space=pltpu.VMEM), pl.BlockSpec(memory_space=pl.ANY)
    smem = pl.BlockSpec(memory_space=pltpu.SMEM)
    room = (4 * len(slots) + 4) * rows
    shapes = []
    for unit in units:
        for dtype in (jnp.float32, jnp.bfloat16):
            shapes.append(jax.ShapeDtypeStruct((2 * len(unit) * rows, width), dtype))
    return pl.pallas_call(
        functools.partial(expert_kernel, slots, units),
        out_shape=tuple(shapes),
        in_specs=[smem, smem, vmem] + [vmem] * len(parts) + [anywhere] * 4,
        out_specs=(vmem,) * len(shapes),
        scratch_shapes=[
            pltpu.VMEM((2, 2, width, 2 * hidden_units), jnp.bfloat16),
            pltpu.VMEM((2, 2 * hidden_units, width), jnp.bfloat16),
            pltpu.VMEM((room, width + LANES), jnp.bfloat16),
            pltpu.VMEM((room, 2 * hidden_units), jnp.bfloat16),
            pltpu.VMEM((room, width), jnp.float32),
            pltpu.SemaphoreType.DMA((2, 2, 3)),
        ],
        compiler_params=pltpu.CompilerParams(vmem_limit_bytes=36 * MIB),
        name="experts",
    )(place, kinds, pick, *parts, *weights)


def attention_kernel(head_dim, group, kv_count, resumes, ends, q_ref, *refs):
    kv_refs, refs = refs[:kv_count], refs[kv_count:]
    if resumes:
        stats_in, mixed_in, refs = refs[0], refs[1], refs[2:]
    rows = q_ref.shape[0]
    kv_heads = kv_refs[0].shape[1] // (2 * head_dim)
    step = max(1, KEYS_AT_ONCE // kv_refs[0].shape[0])
    scale = head_dim**-0.5 * LOG2_E

    def columns(ref, head, count=1):
        return ref[:, pl.ds(pl.multiple_of(head * head_dim, head_dim), count * head_dim)]

    def one_group(g, carry):
        wide = columns(q_ref, group * g, group)
        q = jnp.concatenate(
            [wide[:, i * head_dim : (i + 1) * head_dim] for i in range(group)], axis=0
        )
        peak, total, mixed = None, 0.0, 0.0
        if resumes:
            peak, total, mixed = stats_in[g, 0:1], stats_in[g, 1:2], mixed_in[g]
        for at in range(0, kv_count, step):
            scores = [
                lax.dot_general(
                    columns(ref, g), q, (((1,), (1,)), ((), ())), preferred_element_type=jnp.float32
                )
                for ref in kv_refs[at : at + step]
            ]
            peaks = [jnp.max(s, axis=0, keepdims=True) for s in scores]
            if peak is not None:
                before = peak
                peak = functools.reduce(jnp.maximum, peaks + [before])
                shrink = jnp.exp2((before - peak) * scale)
                total, mixed = total * shrink, mixed * shrink
            else:
                peak = functools.reduce(jnp.maximum, peaks)
            for s, ref in zip(scores, kv_refs[at : at + step]):
                p = jnp.exp2((s - peak) * scale)
                total = total + jnp.sum(p, axis=0, keepdims=True)
                mixed = mixed + lax.dot_general(
                    columns(ref, kv_heads + g),
                    p.astype(jnp.bfloat16),
                    (((0,), (0,)), ((), ())),
                    preferred_element_type=jnp.float32,
                )
        if ends:
            out = (mixed / total).T.astype(jnp.bfloat16)
            at = pl.multiple_of(group * g * head_dim, group * head_dim)
            refs[0][:, pl.ds(at, group * head_dim)] = jnp.concatenate(
                [out[i * rows : (i + 1) * rows] for i in range(group)], axis=1
            )
        else:
            refs[0][g, 0:1] = peak
            refs[0][g, 1:2] = total
            refs[1][g] = mixed
        return carry

    lax.fori_loop(0, kv_heads, one_group, 0, unroll=kv_heads if kv_count <= step else 1)


def attention_call(queries, kv_parts, head_dim, group, state, ends):
    vmem = pl.BlockSpec(memory_space=pltpu.VMEM)
    rows, width = queries.shape
    keys = sum(part.shape[0] for part in kv_parts)
    kv_heads = width // (head_dim * group)
    shapes = (jax.ShapeDtypeStruct((rows, width), jnp.bfloat16),)
    if not ends:
        shapes = (
            jax.ShapeDtypeStruct((kv_heads, 8, group * rows), jnp.float32),
            jax.ShapeDtypeStruct((kv_heads, head_dim, group * rows), jnp.float32),
        )
    state = state or ()
    return pl.pallas_call(
        functools.partial(attention_kernel, head_dim, group, len(kv_parts), bool(state), ends),
        out_shape=shapes,
        in_specs=[vmem] * (1 + len(kv_parts) + len(state)),
        out_specs=(vmem,) * len(shapes),
        compiler_params=pltpu.CompilerParams(vmem_limit_bytes=48 * MIB),
        cost_estimate=pl.CostEstimate(
            flops=4 * rows * keys * width,
            bytes_accessed=4 * rows * width,
            transcendentals=rows * keys * width // head_dim,
        ),
        name="attention",
    )(queries, *kv_parts, *state)


def body(
    hidden_in,
    modality,
    expert_ids,
    route_weights,
    w_gate_up,
    w_down,
    norm_gain,
    w_query,
    key_value_weight,
    q_gain,
    k_gain,
):
    tok_rows, model_width = hidden_in.shape
    groups = lax.axis_size("expert")
    me, core = lax.axis_index("expert"), lax.axis_index("half")
    slots = groups // 4
    slot_order = [0] + list(range(2, slots, 2)) + list(range(1, slots, 2))
    slot_groups = [[s, s + 2] for s in range(0, slots, 4)] + [[s, s + 2] for s in range(1, slots, 4)]

    payload = payload_call(core[None], hidden_in, expert_ids, route_weights, groups)
    lane = jnp.arange(LANES, dtype=jnp.int32)
    pick = ((lane == me) | (lane == me + groups)).astype(jnp.float32)[None, :]
    kinds = modality.reshape(groups, tok_rows)[:, 0]
    place = jnp.stack([me, core]).astype(jnp.int32)

    arrived = {0: payload}
    for s in range(1, slots):
        arrived[s] = swap(payload, 4 * s, 4 * s)
    own_gu = w_gate_up.transpose(0, 2, 1, 3)
    weights = (own_gu, swap_half(own_gu), w_down, swap_half(w_down))

    jobs = []

    def cross(value, *masks):
        if len(jobs) > 1:
            value = after(value, jobs[-2])
        jobs.append(swap(value, *masks))
        return jobs[-1]

    two, four, outs, returned = {}, {}, {}, {}

    def collect(members, last):
        for s in members:
            two[s] = jnp.concatenate([arrived[s], cross(arrived[s], 1, 2)], axis=0)
            if last is not None and s == members[-1]:
                two[s] = after(two[s], last)
            four[s] = cross(two[s], 2, 1)

    def work(members):
        units = [[s] for s in reversed(members)]
        parts = [part for s in members for part in (two[s], four[s])]
        found = expert_call(members, units, place, kinds, pick, parts, weights)
        for u, unit in enumerate(units):
            outs[unit[0]] = found[2 * u : 2 * u + 2]
        return found[0]

    def give_back(members):
        for s in reversed(members):
            keep, send = outs[s]
            keep = keep + swap(send, 2, 1).astype(jnp.float32)
            cut = keep.shape[0] // 2
            back = swap(keep[cut:].astype(jnp.bfloat16), 1, 2)
            returned[s] = keep[:cut] + back.astype(jnp.float32)

    collect(slot_groups[0], None)
    for before, members in zip(slot_groups, slot_groups[1:]):
        collect(members, work(before))
        give_back(before)
    work(slot_groups[-1])
    give_back(slot_groups[-1])
    mixture = returned[0]
    for s in range(1, slots):
        mixture = mixture + swap(returned[s].astype(jnp.bfloat16), 4 * s, 4 * s).astype(jnp.float32)
    mine = payload[:, :model_width].astype(jnp.float32) + mixture
    theirs = swap_half(mine)
    hidden_out = jnp.where(
        core == 0,
        jnp.concatenate([mine, theirs], axis=0),
        jnp.concatenate([theirs, mine], axis=0),
    )

    normed = rms_scale(hidden_out, norm_gain).astype(jnp.bfloat16)
    head_dim = q_gain.shape[0]
    kv_width = key_value_weight.shape[2]
    kv_heads = kv_width // head_dim
    key_value = jnp.dot(
        normed,
        key_value_weight.reshape(model_width, 2 * kv_width),
        preferred_element_type=jnp.float32,
    )
    keys = rms_scale(key_value[:, :kv_width].reshape(tok_rows, kv_heads, head_dim), k_gain)
    own_kv = jnp.concatenate(
        [keys.reshape(tok_rows, kv_width), key_value[:, kv_width:]], axis=1
    ).astype(jnp.bfloat16)
    queries = jnp.dot(normed, w_query, preferred_element_type=jnp.float32)
    heads = queries.shape[1] // head_dim
    queries = rms_scale(queries.reshape(tok_rows, heads, head_dim), q_gain)
    queries = queries.reshape(tok_rows, heads * head_dim).astype(jnp.bfloat16)

    arrived, bit = {0: own_kv}, slots // 2
    while bit:
        for s in sorted(arrived):
            arrived[s + bit] = swap(arrived[s], 4 * bit, 4 * bit)
        bit //= 2
    kv_parts = []
    for s in slot_order:
        pair = jnp.concatenate([arrived[s], swap(arrived[s], 1, 2)], axis=0)
        kv_parts += [pair, swap(pair, 2, 1)]
    state = attention_call(queries, kv_parts[:-4], head_dim, heads // kv_heads, None, False)
    (attended,) = attention_call(queries, kv_parts[-4:], head_dim, heads // kv_heads, state, True)
    return hidden_out, attended


def solution(mesh):
    in_specs = (
        P("expert", None),
        P(),
        P("expert", None),
        P("expert", None),
        P("expert", None, None, "half"),
        P("expert", "half", None),
        P(),
        P(None, "half"),
        P(None, None, "half"),
        P(),
        P(),
    )
    out_specs = (P("expert", None), P("expert", "half"))
    return jax.shard_map(body, mesh=mesh, in_specs=in_specs, out_specs=out_specs, check_vma=False)
```
